32 devices in a mesh: grid: 4 (over z), patch: 4 (over y, x), cross: 2 (over core).
Axes of the slice: x: 2, y: 2, z: 4, core: 2. Of those that a mesh axis runs over, the one named last changes fastest.
Arguments:
- adjoint_now: float32 [3, 4, 32, 16, 128], P(None, 'grid', 'patch', 'cross'), may hold values from -6 to 6
- adjoint_prev: float32 [3, 4, 32, 16, 128], P(None, 'grid', 'patch', 'cross'), may hold values from -6 to 6
- stiffness: float32 [4, 32, 16, 128], P('grid', 'patch', 'cross'), may hold values from 0.08 to 0.3
- adjoint_source: bfloat16 [2, 3, 4, 32, 16, 128], P(None, None, 'grid', 'patch', 'cross'), may hold values from -6 to 6
- forward_field: bfloat16 [2, 3, 4, 32, 16, 128], P(None, None, 'grid', 'patch', 'cross'), may hold values from -6 to 6
- material_mask: int32 [4, 4, 2], P('grid', 'patch', 'cross'), may hold values 0 or 1
- interface_map: int32 [4, 32, 16], P('grid', 'patch', 'cross'), may hold values from 0 to 63, as said below
Outputs:
- adjoint_final: float32 [3, 4, 32, 16, 128], P(None, 'grid', 'patch', 'cross')
- kernel: float32 [4, 32, 16, 128], P('grid', 'patch', 'cross')
The draws below stay inside these ranges and needn't reach their ends.
Inputs may be any that keep to these rules, and one draw needn't show every extreme that they name: `interface_map`: each value indexes a column of the same patch's plane of 8 x 8 cells, row-major, at most one cell away from the cell's own position along each horizontal dimension; the first and last cells of each patch are fed by their own column.
All inputs are finite; a program needn't handle non-finite values. No bound on the sum of `material_mask` on one device may be relied on, other than what follows from the above.
Results may differ from the reference program's by a relative error of at most 0.00035.
Values sent between devices are 32-bit elements; how exact they have to be, the bound alone decides.
A program may use at most 64 MiB of HBM per device.

```python
import math
import jax
import jax.numpy as jnp

CX = 8
CY = 8
CZ = 128
STEPS = 2
GRIDS = 4
PATCHES = 4
CROSSES = 2
PX = 32
PY = 16


def draw_interface_map(key, part):
    first_key = jax.random.fold_in(key, 11)
    second_key = jax.random.fold_in(key, 12)
    step_rows = jax.random.randint(first_key, (GRIDS, PX, PY), -1, 2)
    step_cols = jax.random.randint(second_key, (GRIDS, PX, PY), -1, 2)
    local_rows = (jnp.arange(PX, dtype=jnp.int32) % CX)[None, :, None]
    local_cols = (jnp.arange(PY, dtype=jnp.int32) % CY)[None, None, :]
    moved_rows = jnp.clip(local_rows + step_rows, 0, CX - 1)
    moved_cols = jnp.clip(local_cols + step_cols, 0, CY - 1)
    corner = (local_rows == 0) & (local_cols == 0) | (local_rows == CX - 1) & (local_cols == CY - 1)
    final_rows = jnp.where(corner, local_rows, moved_rows)
    final_cols = jnp.where(corner, local_cols, moved_cols)
    return (final_rows * CY + final_cols).astype(jnp.int32)


def touch_ends(values, rng, smallest, high):
    dims = values.shape
    spot = [jax.random.randint(jax.random.fold_in(rng, axis), (), 0, dims[axis]) for axis in range(len(dims))]
    values = values.at[tuple(spot)].set(smallest)
    longest = dims.index(max(dims))
    spot[longest] = (spot[longest] + 1) % dims[longest]
    return values.at[tuple(spot)].set(high)


def block_scale(rng, extent, cuts, low, top_value):
    def one(dim, parts):
        steps = jax.random.uniform(jax.random.fold_in(jax.random.fold_in(rng, 6), dim), (parts,), jnp.float32, low / len(cuts), top_value / len(cuts))
        return jnp.repeat(jnp.exp(steps), extent[dim] // parts).reshape((-1,) + (1,) * (len(extent) - dim - 1))

    gain = one(*cuts[0])
    for cut in cuts[1:]:
        gain = gain * one(*cut)
    return gain


def bell_draw(own_key, shape, spread, most, shards=(), kind=jnp.bfloat16):
    array = spread * jax.random.normal(own_key, shape, jnp.float32)
    if shards:
        array = array * block_scale(own_key, shape, shards, -0.22, 0.18)
    return jnp.clip(array, -most, most).astype(kind)


def setup_inputs(seed: int = 0) -> dict:
    key_of = jax.random.split(jax.random.key(seed), 8)
    adjoint_now = bell_draw(key_of[0], (3, GRIDS, PX, PY, CZ), 1.0, 6.0, ((1, 4), (2, 4), (3, 2)), jnp.float32)
    adjoint_prev = bell_draw(key_of[1], (3, GRIDS, PX, PY, CZ), 1.0, 6.0, ((1, 4), (2, 4), (3, 2)), jnp.float32)
    stiffness = jnp.clip(jnp.exp(math.log(0.3) - 1.3217559 * jax.random.uniform(key_of[2], (GRIDS, PX, PY, CZ), jnp.float32) ** block_scale(key_of[2], (GRIDS, PX, PY, CZ), ((0, 4), (1, 4), (2, 2)), -0.2, 0.2)), 0.08, 0.3)
    adjoint_source = bell_draw(key_of[3], (STEPS, 3, GRIDS, PX, PY, CZ), 1.0, 6.0, ((2, 4), (3, 4), (4, 2)))
    forward_field = bell_draw(key_of[4], (STEPS, 3, GRIDS, PX, PY, CZ), 1.0, 6.0, ((2, 4), (3, 4), (4, 2)))
    material_mask = touch_ends((jax.random.randint(key_of[5], (GRIDS, PATCHES, CROSSES), 0, 4) < 3).astype(jnp.int32), jax.random.fold_in(key_of[5], 1), 0, 1)
    interface_map = draw_interface_map(jax.random.fold_in(key_of[7], 71), 0)
    return dict(adjoint_now=adjoint_now, adjoint_prev=adjoint_prev, stiffness=stiffness, adjoint_source=adjoint_source, forward_field=forward_field, material_mask=material_mask, interface_map=interface_map)


def lap_field(field, material_rows, material_cols, grid_ids):
    bottom = field[:, :, :, :, -1]
    above = jnp.concatenate([jnp.zeros_like(bottom[:, :1]), bottom[:, :-1]], axis=1)
    mapped = above[:, grid_ids, material_rows, material_cols]
    top_plane = jnp.where(grid_ids == 0, field[:, :, :, :, 0], mapped)
    first = field[:, :, :, :, 0]
    below_plane = jnp.concatenate([first[:, 1:], jnp.zeros_like(first[:, :1])], axis=1)
    upper = jnp.concatenate([top_plane[..., None], field[..., :-1]], axis=4)
    lower = jnp.concatenate([field[..., 1:], below_plane[..., None]], axis=4)
    beside = jnp.roll(field, 1, axis=2) + jnp.roll(field, -1, axis=2)
    beside = beside + jnp.roll(field, 1, axis=3) + jnp.roll(field, -1, axis=3)
    return beside + upper + lower - 6.0 * field


def reference(adjoint_now, adjoint_prev, stiffness, adjoint_source, forward_field, material_mask, interface_map):
    grid_count = interface_map.shape[0]
    rows_all = interface_map.shape[1]
    cols_all = interface_map.shape[2]
    base_rows = (jnp.arange(rows_all, dtype=jnp.int32) // CX * CX)[None, :, None]
    base_cols = (jnp.arange(cols_all, dtype=jnp.int32) // CY * CY)[None, None, :]
    row_index = (base_rows + interface_map // CY).astype(jnp.int32)
    col_index = (base_cols + interface_map % CY).astype(jnp.int32)
    grid_ids = jnp.broadcast_to(jnp.arange(grid_count, dtype=jnp.int32)[:, None, None], interface_map.shape)
    cell_mask = jnp.repeat(jnp.repeat(material_mask, CX, axis=1), CY, axis=2).astype(jnp.float32)[:, :, :, None]
    field = adjoint_now
    older = adjoint_prev
    kernel = jnp.zeros(stiffness.shape, jnp.float32)
    for step in range(STEPS):
        slot = STEPS - 1 - step
        lap = lap_field(field, row_index, col_index, grid_ids)
        fresh = (2.0 * field - older + stiffness * lap + adjoint_source[slot].astype(jnp.float32)) * cell_mask
        kernel = kernel + jnp.sum(fresh * forward_field[slot].astype(jnp.float32), axis=0)
        older = field
        field = fresh
    return field, kernel
```

```python
import functools

import jax
import jax.numpy as jnp
from jax import lax
from jax.experimental import pallas as pl
from jax.experimental.pallas import tpu as pltpu
from jax.sharding import PartitionSpec as P

MESH = pl.DeviceIdType.MESH
F32 = jnp.float32


def lane_roll(value, by):
    return pltpu.roll(value, by % value.shape[-1], value.ndim - 1)


def row_roll(value, by):
    return pltpu.roll(value, by % value.shape[-2], value.ndim - 2)


def kernel(
    grids, patches, u_hbm, w_hbm, k_hbm, s_hbm, f_hbm, m_hbm, i_hbm, out_ref, kern_ref,
    u_v, w_v, k_v, s_v, f_v, m_v, i_v, side_x, side_y, plane, got_x, got_y, got_z,
    load_sem, send_sem, recv_sem,
):
    g = lax.axis_index("grid")
    p = lax.axis_index("patch")
    q = lax.axis_index("cross")
    p_next = lax.rem(p + 1, patches)
    p_prev = lax.rem(p + patches - 1, patches)
    not_top = g > 0
    not_last = g < grids - 1

    barrier = pltpu.get_barrier_semaphore()
    pl.semaphore_signal(barrier, inc=1, device_id={"patch": p_next}, device_id_type=MESH)
    pl.semaphore_signal(barrier, inc=1, device_id={"patch": p_prev}, device_id_type=MESH)
    pl.semaphore_signal(barrier, inc=1, device_id={"cross": 1 - q}, device_id_type=MESH)

    @pl.when(not_top)
    def _():
        pl.semaphore_signal(barrier, inc=1, device_id={"grid": g - 1}, device_id_type=MESH)

    @pl.when(not_last)
    def _():
        pl.semaphore_signal(barrier, inc=1, device_id={"grid": g + 1}, device_id_type=MESH)

    pairs = ((u_hbm, u_v), (i_hbm, i_v), (m_hbm, m_v), (w_hbm, w_v), (k_hbm, k_v), (s_hbm, s_v), (f_hbm, f_v))
    loads = [pltpu.make_async_copy(a, b, load_sem.at[n]) for n, (a, b) in enumerate(pairs)]
    for load in loads:
        load.start()

    nc, nx, ny, nz = u_v.shape[0], u_v.shape[2], u_v.shape[3], u_v.shape[4]
    lane = lax.broadcasted_iota(jnp.int32, (ny, nz), 1)
    row = lax.broadcasted_iota(jnp.int32, (ny, nz), 0)
    odd = lax.rem(lane, 2) == 1

    @pl.when(jnp.logical_not(not_top))
    def _():
        got_z[:, 0] = jnp.zeros((2, ny, nz), F32)

    @pl.when(jnp.logical_not(not_last))
    def _():
        got_z[:, 1] = jnp.zeros((2, ny, nz), F32)

    def copies(step):
        def remote(src, dst, n, device):
            return pltpu.make_async_remote_copy(
                src_ref=src, dst_ref=dst, send_sem=send_sem.at[step, n], recv_sem=recv_sem.at[step, n],
                device_id=device, device_id_type=MESH,
            )

        return (
            remote(side_x.at[step, 1], got_x.at[step, 0], 0, {"patch": p_next}),
            remote(side_x.at[step, 0], got_x.at[step, 1], 1, {"patch": p_prev}),
            remote(side_y.at[step], got_y.at[step], 2, {"cross": 1 - q}),
            remote(plane.at[step], got_z.at[step, 0], 3, {"grid": g + 1}),
            remote(plane.at[step], got_z.at[step, 1], 4, {"grid": g - 1}),
        )

    def pack(step, u):
        side_x[step, 0] = u[:, 0]
        side_x[step, 1] = u[:, nx - 1]
        for c in range(nc):
            for x in range(nx):
                side_y[step, 0, c, x : x + 1] = u[c, x, ny - 1 : ny]
                side_y[step, 1, c, x : x + 1] = u[c, x, 0:1]
        packed = jnp.zeros((ny, nz), F32)
        for c in range(nc):
            for x in range(nx):
                k = c * nx + x
                packed = jnp.where(lax.div(lane, 2) == k, lane_roll(u[c, x], 2 * k + 1), packed)
        plane[step] = packed
        return packed

    def send(step):
        down, up = copies(step)[3:]

        @pl.when(not_last)
        def _():
            down.start()

        @pl.when(not_top)
        def _():
            up.start()

        for copy in copies(step)[:3]:
            copy.start()

    def receive(step):
        for copy in copies(step)[:3]:
            copy.wait_recv()
        down, up = copies(step)[3:]

        @pl.when(not_top)
        def _():
            down.wait_recv()

        @pl.when(not_last)
        def _():
            up.wait_recv()

    def finish(step):
        for copy in copies(step)[:3]:
            copy.wait_send()
        down, up = copies(step)[3:]

        @pl.when(not_last)
        def _():
            down.wait_send()

        @pl.when(not_top)
        def _():
            up.wait_send()

    def inner(u):
        none = jnp.zeros((nc, 1, ny, nz), F32)
        total = jnp.concatenate([u[:, 1:], none], axis=1) + jnp.concatenate([none, u[:, :-1]], axis=1)
        parts = []
        for c in range(nc):
            line = []
            for x in range(nx):
                cell = u[c, x]
                zs = jnp.where(lane == 0, 0.0, lane_roll(cell, 1)) + jnp.where(lane == nz - 1, 0.0, lane_roll(cell, -1))
                ys = jnp.where(row == 0, 0.0, row_roll(cell, 1)) + jnp.where(row == ny - 1, 0.0, row_roll(cell, -1))
                line.append(zs + ys)
            parts.append(jnp.stack(line))
        return total + jnp.stack(parts) - 6.0 * u

    def outer(step, packed, feeds):
        above = lane_roll(got_z[step, 0], 1)
        below = jnp.where(not_last, lane_roll(got_z[step, 1], -1), 0.0)
        fed = above
        for dx, dy, mask in feeds:
            moved = row_roll(above, -dy) if dy else above
            moved = lane_roll(moved, -2 * dx) if dx else moved
            fed = jnp.where(mask, moved, fed)
        ghost = jnp.where(odd, jnp.where(not_top, fed, packed), below)
        parts = []
        for c in range(nc):
            line = []
            for x in range(nx):
                k = c * nx + x
                zs = jnp.where((lane == 0) | (lane == nz - 1), lane_roll(ghost, -(2 * k + 1)), 0.0)
                first = jnp.broadcast_to(got_y[step, 0, c, x : x + 1], (ny, nz))
                last = jnp.broadcast_to(got_y[step, 1, c, x : x + 1], (ny, nz))
                ys = jnp.where(row == 0, first, jnp.where(row == ny - 1, last, 0.0))
                total = zs + ys
                if x == 0:
                    total = total + got_x[step, 0, c]
                if x == nx - 1:
                    total = total + got_x[step, 1, c]
                line.append(total)
            parts.append(jnp.stack(line))
        return jnp.stack(parts)

    loads[0].wait()
    u0 = u_v[:, 0]
    packed0 = pack(0, u0)
    pl.semaphore_wait(barrier, 3 + not_top.astype(jnp.int32) + not_last.astype(jnp.int32))
    send(0)

    loads[1].wait()
    own = i_v[0].astype(F32)
    spread = (lax.rem(lax.div(lax.broadcasted_iota(jnp.int32, (nz, nx), 0), 2), nx)
              == lax.broadcasted_iota(jnp.int32, (nz, nx), 1)).astype(F32)
    eye = (lax.broadcasted_iota(jnp.int32, (ny, ny), 0) == lax.broadcasted_iota(jnp.int32, (ny, ny), 1)).astype(F32)
    tall = jnp.dot(spread, own, preferred_element_type=F32)
    source = lax.dot_general(eye, tall, (((1,), (1,)), ((), ())), preferred_element_type=F32)
    here = lax.rem(lax.div(lane, 2), nx)
    feeds = []
    for dx in (-1, 0, 1):
        for dy in (-1, 0, 1):
            if dx or dy:
                feeds.append((dx, dy, source == ((here + dx) * ny + row + dy).astype(F32)))

    for load in loads[2:]:
        load.wait()
    mask = m_v[0, 0, 0].astype(F32)
    stiff = k_v[0] * mask
    base = (2.0 * u0 - w_v[:, 0] + s_v[1, :, 0].astype(F32)) * mask + stiff[None] * inner(u0)
    receive(0)
    u1 = base + stiff[None] * outer(0, packed0, feeds)
    packed1 = pack(1, u1)
    send(1)
    kern = jnp.sum(u1 * f_v[1, :, 0].astype(F32), axis=0)
    base = (2.0 * u1 - u0 + s_v[0, :, 0].astype(F32)) * mask + stiff[None] * inner(u1)
    receive(1)
    u2 = base + stiff[None] * outer(1, packed1, feeds)
    out_ref[:, 0] = u2
    kern_ref[0] = kern + jnp.sum(u2 * f_v[0, :, 0].astype(F32), axis=0)
    finish(0)
    finish(1)


def solution(mesh):
    grids, patches = mesh.shape["grid"], mesh.shape["patch"]

    def local(now, prev, stiffness, source, forward, mask, feed):
        nc, _, nx, ny, nz = now.shape
        args = (now, prev, stiffness, source, forward, mask, feed)
        vmem = [pltpu.VMEM(a.shape, a.dtype) for a in args]
        vmem[5] = pltpu.SMEM(mask.shape, mask.dtype)
        return pl.pallas_call(
            functools.partial(kernel, grids, patches),
            out_shape=(jax.ShapeDtypeStruct(now.shape, F32), jax.ShapeDtypeStruct(stiffness.shape, F32)),
            in_specs=[pl.BlockSpec(memory_space=pl.ANY)] * 7,
            out_specs=[pl.BlockSpec(memory_space=pltpu.VMEM)] * 2,
            scratch_shapes=vmem + [
                pltpu.VMEM((2, 2, nc, ny, nz), F32),
                pltpu.VMEM((2, 2, nc, nx, nz), F32),
                pltpu.VMEM((2, ny, nz), F32),
                pltpu.VMEM((2, 2, nc, ny, nz), F32),
                pltpu.VMEM((2, 2, nc, nx, nz), F32),
                pltpu.VMEM((2, 2, ny, nz), F32),
                pltpu.SemaphoreType.DMA((7,)),
                pltpu.SemaphoreType.DMA((2, 5)),
                pltpu.SemaphoreType.DMA((2, 5)),
            ],
            compiler_params=pltpu.CompilerParams(collective_id=0, has_side_effects=True),
        )(*args)

    in_specs = (
        P(None, "grid", "patch", "cross", None),
        P(None, "grid", "patch", "cross", None),
        P("grid", "patch", "cross", None),
        P(None, None, "grid", "patch", "cross", None),
        P(None, None, "grid", "patch", "cross", None),
        P("grid", "patch", "cross"),
        P("grid", "patch", "cross"),
    )
    out_specs = (P(None, "grid", "patch", "cross", None), P("grid", "patch", "cross", None))
    return jax.shard_map(local, mesh=mesh, in_specs=in_specs, out_specs=out_specs, check_vma=False)
```

```python
import functools

import jax
import jax.numpy as jnp
from jax import lax
from jax.experimental import pallas as pl
from jax.experimental.pallas import tpu as pltpu
from jax.sharding import PartitionSpec as P

MESH = pl.DeviceIdType.MESH
F32 = jnp.float32


def lane_roll(value, by):
    return pltpu.roll(value, by % value.shape[-1], value.ndim - 1)


def row_roll(value, by):
    return pltpu.roll(value, by % value.shape[-2], value.ndim - 2)


def kernel(
    grids, patches, u_hbm, w_hbm, k_hbm, s_hbm, f_hbm, m_hbm, i_hbm, out_ref, kern_ref,
    u_v, w_v, k_v, s_v, f_v, m_v, i_v, side_x, side_y, plane, got_x, got_y, got_z,
    load_sem, send_sem, recv_sem,
):
    g = lax.axis_index("grid")
    p = lax.axis_index("patch")
    q = lax.axis_index("cross")
    p_next = lax.rem(p + 1, patches)
    p_prev = lax.rem(p + patches - 1, patches)
    not_top = g > 0
    not_last = g < grids - 1

    barrier = pltpu.get_barrier_semaphore()
    pl.semaphore_signal(barrier, inc=1, device_id={"patch": p_next}, device_id_type=MESH)
    pl.semaphore_signal(barrier, inc=1, device_id={"patch": p_prev}, device_id_type=MESH)
    pl.semaphore_signal(barrier, inc=1, device_id={"cross": 1 - q}, device_id_type=MESH)

    @pl.when(not_top)
    def _():
        pl.semaphore_signal(barrier, inc=1, device_id={"grid": g - 1}, device_id_type=MESH)

    @pl.when(not_last)
    def _():
        pl.semaphore_signal(barrier, inc=1, device_id={"grid": g + 1}, device_id_type=MESH)

    pairs = ((u_hbm, u_v), (i_hbm, i_v), (m_hbm, m_v), (w_hbm, w_v), (k_hbm, k_v), (s_hbm, s_v), (f_hbm, f_v))
    loads = [pltpu.make_async_copy(a, b, load_sem.at[n]) for n, (a, b) in enumerate(pairs)]
    for load in loads:
        load.start()

    nc, nx, ny, nz = u_v.shape[0], u_v.shape[2], u_v.shape[3], u_v.shape[4]
    lane = lax.broadcasted_iota(jnp.int32, (ny, nz), 1)
    row = lax.broadcasted_iota(jnp.int32, (ny, nz), 0)
    odd = lax.rem(lane, 2) == 1

    @pl.when(jnp.logical_not(not_top))
    def _():
        got_z[:, 0] = jnp.zeros((2, ny, nz), F32)

    @pl.when(jnp.logical_not(not_last))
    def _():
        got_z[:, 1] = jnp.zeros((2, ny, nz), F32)

    def copies(step):
        def remote(src, dst, n, device):
            return pltpu.make_async_remote_copy(
                src_ref=src, dst_ref=dst, send_sem=send_sem.at[step, n], recv_sem=recv_sem.at[step, n],
                device_id=device, device_id_type=MESH,
            )

        return (
            remote(side_x.at[step, 1], got_x.at[step, 0], 0, {"patch": p_next}),
            remote(side_x.at[step, 0], got_x.at[step, 1], 1, {"patch": p_prev}),
            remote(side_y.at[step], got_y.at[step], 2, {"cross": 1 - q}),
            remote(plane.at[step], got_z.at[step, 0], 3, {"grid": g + 1}),
            remote(plane.at[step], got_z.at[step, 1], 4, {"grid": g - 1}),
        )

    def pack(step, u):
        side_x[step, 0] = u[:, 0]
        side_x[step, 1] = u[:, nx - 1]
        for c in range(nc):
            for x in range(nx):
                side_y[step, 0, c, x : x + 1] = u[c, x, ny - 1 : ny]
                side_y[step, 1, c, x : x + 1] = u[c, x, 0:1]
        packed = jnp.zeros((ny, nz), F32)
        for c in range(nc):
            for x in range(nx):
                k = c * nx + x
                packed = jnp.where(lax.div(lane, 2) == k, lane_roll(u[c, x], 2 * k + 1), packed)
        plane[step] = packed
        return packed

    def send(step):
        down, up = copies(step)[3:]

        @pl.when(not_last)
        def _():
            down.start()

        @pl.when(not_top)
        def _():
            up.start()

        for copy in copies(step)[:3]:
            copy.start()

    def receive(step):
        for copy in copies(step)[:3]:
            copy.wait_recv()
        down, up = copies(step)[3:]

        @pl.when(not_top)
        def _():
            down.wait_recv()

        @pl.when(not_last)
        def _():
            up.wait_recv()

    def finish(step):
        for copy in copies(step)[:3]:
            copy.wait_send()
        down, up = copies(step)[3:]

        @pl.when(not_last)
        def _():
            down.wait_send()

        @pl.when(not_top)
        def _():
            up.wait_send()

    def inner(u):
        none = jnp.zeros((nc, 1, ny, nz), F32)
        total = jnp.concatenate([u[:, 1:], none], axis=1) + jnp.concatenate([none, u[:, :-1]], axis=1)
        parts = []
        for c in range(nc):
            line = []
            for x in range(nx):
                cell = u[c, x]
                zs = jnp.where(lane == 0, 0.0, lane_roll(cell, 1)) + jnp.where(lane == nz - 1, 0.0, lane_roll(cell, -1))
                ys = jnp.where(row == 0, 0.0, row_roll(cell, 1)) + jnp.where(row == ny - 1, 0.0, row_roll(cell, -1))
                line.append(zs + ys)
            parts.append(jnp.stack(line))
        return total + jnp.stack(parts) - 6.0 * u

    def outer(step, packed, feeds):
        above = lane_roll(got_z[step, 0], 1)
        below = jnp.where(not_last, lane_roll(got_z[step, 1], -1), 0.0)
        fed = above
        for dx, dy, mask in feeds:
            moved = row_roll(above, -dy) if dy else above
            moved = lane_roll(moved, -2 * dx) if dx else moved
            fed = jnp.where(mask, moved, fed)
        ghost = jnp.where(odd, jnp.where(not_top, fed, packed), below)
        parts = []
        for c in range(nc):
            line = []
            for x in range(nx):
                k = c * nx + x
                zs = jnp.where((lane == 0) | (lane == nz - 1), lane_roll(ghost, -(2 * k + 1)), 0.0)
                first = jnp.broadcast_to(got_y[step, 0, c, x : x + 1], (ny, nz))
                last = jnp.broadcast_to(got_y[step, 1, c, x : x + 1], (ny, nz))
                ys = jnp.where(row == 0, first, jnp.where(row == ny - 1, last, 0.0))
                total = zs + ys
                if x == 0:
                    total = total + got_x[step, 0, c]
                if x == nx - 1:
                    total = total + got_x[step, 1, c]
                line.append(total)
            parts.append(jnp.stack(line))
        return jnp.stack(parts)

    loads[0].wait()
    u0 = u_v[:, 0]
    packed0 = pack(0, u0)
    pl.semaphore_wait(barrier, 3 + not_top.astype(jnp.int32) + not_last.astype(jnp.int32))
    send(0)

    loads[1].wait()
    own = i_v[0].astype(F32)
    spread = (lax.rem(lax.div(lax.broadcasted_iota(jnp.int32, (nz, nx), 0), 2), nx)
              == lax.broadcasted_iota(jnp.int32, (nz, nx), 1)).astype(F32)
    eye = (lax.broadcasted_iota(jnp.int32, (ny, ny), 0) == lax.broadcasted_iota(jnp.int32, (ny, ny), 1)).astype(F32)
    tall = jnp.dot(spread, own, preferred_element_type=F32)
    source = lax.dot_general(eye, tall, (((1,), (1,)), ((), ())), preferred_element_type=F32)
    here = lax.rem(lax.div(lane, 2), nx)
    feeds = []
    for dx in (-1, 0, 1):
        for dy in (-1, 0, 1):
            if dx or dy:
                feeds.append((dx, dy, source == ((here + dx) * ny + row + dy).astype(F32)))

    for load in loads[2:]:
        load.wait()
    mask = m_v[0, 0, 0].astype(F32)
    stiff = k_v[0] * mask
    base = (2.0 * u0 - w_v[:, 0] + s_v[1, :, 0].astype(F32)) * mask + stiff[None] * inner(u0)
    receive(0)
    u1 = base + stiff[None] * outer(0, packed0, feeds)
    packed1 = pack(1, u1)
    send(1)
    kern = jnp.sum(u1 * f_v[1, :, 0].astype(F32), axis=0)
    base = (2.0 * u1 - u0 + s_v[0, :, 0].astype(F32)) * mask + stiff[None] * inner(u1)
    receive(1)
    u2 = base + stiff[None] * outer(1, packed1, feeds)
    out_ref[:, 0] = u2
    kern_ref[0] = kern + jnp.sum(u2 * f_v[0, :, 0].astype(F32), axis=0)
    finish(0)
    finish(1)


def store(field_ref, kern_ref, field_out, kern_out, sem):
    first = pltpu.make_async_copy(field_ref, field_out, sem.at[0])
    second = pltpu.make_async_copy(kern_ref, kern_out, sem.at[1])
    first.start()
    second.start()
    first.wait()
    second.wait()


def solution(mesh):
    grids, patches = mesh.shape["grid"], mesh.shape["patch"]

    def local(now, prev, stiffness, source, forward, mask, feed):
        nc, _, nx, ny, nz = now.shape
        args = (now, prev, stiffness, source, forward, mask, feed)
        vmem = [pltpu.VMEM(a.shape, a.dtype) for a in args]
        vmem[5] = pltpu.SMEM(mask.shape, mask.dtype)
        done = pl.pallas_call(
            functools.partial(kernel, grids, patches),
            out_shape=(pltpu.VMEM(now.shape, F32), pltpu.VMEM(stiffness.shape, F32)),
            in_specs=[pl.BlockSpec(memory_space=pltpu.HBM)] * 7,
            out_specs=[pl.BlockSpec(memory_space=pltpu.VMEM)] * 2,
            scratch_shapes=vmem + [
                pltpu.VMEM((2, 2, nc, ny, nz), F32),
                pltpu.VMEM((2, 2, nc, nx, nz), F32),
                pltpu.VMEM((2, ny, nz), F32),
                pltpu.VMEM((2, 2, nc, ny, nz), F32),
                pltpu.VMEM((2, 2, nc, nx, nz), F32),
                pltpu.VMEM((2, 2, ny, nz), F32),
                pltpu.SemaphoreType.DMA((7,)),
                pltpu.SemaphoreType.DMA((2, 5)),
                pltpu.SemaphoreType.DMA((2, 5)),
            ],
            compiler_params=pltpu.CompilerParams(collective_id=0, has_side_effects=True),
        )(*args)
        return pl.pallas_call(
            store,
            out_shape=(pltpu.HBM(now.shape, F32), pltpu.HBM(stiffness.shape, F32)),
            in_specs=[pl.BlockSpec(memory_space=pl.ANY)] * 2,
            out_specs=[pl.BlockSpec(memory_space=pltpu.HBM)] * 2,
            scratch_shapes=[pltpu.SemaphoreType.DMA((2,))],
        )(*[pltpu.with_memory_space_constraint(d, pltpu.VMEM) for d in done])

    in_specs = (
        P(None, "grid", "patch", "cross", None),
        P(None, "grid", "patch", "cross", None),
        P("grid", "patch", "cross", None),
        P(None, None, "grid", "patch", "cross", None),
        P(None, None, "grid", "patch", "cross", None),
        P("grid", "patch", "cross"),
        P("grid", "patch", "cross"),
    )
    out_specs = (P(None, "grid", "patch", "cross", None), P("grid", "patch", "cross", None))
    return jax.shard_map(local, mesh=mesh, in_specs=in_specs, out_specs=out_specs, check_vma=False)
```

```python
import functools

import jax
import jax.numpy as jnp
from jax import lax
from jax.experimental import pallas as pl
from jax.experimental.pallas import tpu as pltpu
from jax.sharding import PartitionSpec as P

MESH = pl.DeviceIdType.MESH
F32 = jnp.float32


def lane_roll(value, by):
    return pltpu.roll(value, by % value.shape[-1], value.ndim - 1)


def row_roll(value, by):
    return pltpu.roll(value, by % value.shape[-2], value.ndim - 2)


def kernel(
    grids, patches, u_hbm, w_hbm, k_hbm, s_hbm, f_hbm, m_ref, i_hbm, out_ref, kern_ref,
    u_v, w_v, k_v, s_v, f_v, i_v, side_y, out_p, out_g, out_c, got_y, got_p, got_g, got_d, got_q, got_c,
    load_sem, send_sem, recv_sem,
):
    g = lax.axis_index("grid")
    p = lax.axis_index("patch")
    q = lax.axis_index("cross")
    nxt = lax.rem(p + 1, patches)
    prv = lax.rem(p + patches - 1, patches)
    far = 1 - q
    not_top = g > 0
    not_last = g < grids - 1

    flat = (
        (out_p.at[1], got_p.at[0], (g, nxt, q)),
        (out_p.at[0], got_p.at[1], (g, prv, q)),
        (out_c.at[1], got_c.at[0], (g, nxt, far)),
        (out_c.at[0], got_c.at[1], (g, prv, far)),
        (side_y.at[0], got_y.at[0], (g, p, far)),
        (side_y.at[1], got_y.at[1], (g, p, far)),
    )

    def vertical(slot, other):
        return (
            (out_g, got_g.at[slot], (other, p, q)),
            (out_g.at[0], got_d.at[0, slot], (other, nxt, q)),
            (out_g.at[0], got_d.at[1, slot], (other, prv, q)),
            (out_g.at[0], got_q.at[slot], (other, p, far)),
        )

    down, up = vertical(0, g + 1), vertical(1, g - 1)

    def run(messages, first, what):
        for n, (src, dst, device) in enumerate(messages):
            copy = pltpu.make_async_remote_copy(
                src_ref=src, dst_ref=dst, send_sem=send_sem.at[first + n], recv_sem=recv_sem.at[first + n],
                device_id=device, device_id_type=MESH,
            )
            getattr(copy, what)()

    barrier = pltpu.get_barrier_semaphore()

    def greet(messages):
        for _, _, device in messages:
            pl.semaphore_signal(barrier, inc=1, device_id=device, device_id_type=MESH)

    def both(condition, body):
        @pl.when(condition)
        def _():
            body()

    greet(flat[:5])
    both(not_last, lambda: greet(down))
    both(not_top, lambda: greet(up))

    pairs = ((u_hbm, u_v), (w_hbm, w_v), (k_hbm, k_v), (s_hbm, s_v), (i_hbm, i_v), (f_hbm, f_v))
    loads = [pltpu.make_async_copy(a, b, load_sem.at[n]) for n, (a, b) in enumerate(pairs)]
    for load in loads:
        load.start()

    nc, nx, ny, nz = u_v.shape[0], u_v.shape[2], u_v.shape[3], u_v.shape[4]
    lane = lax.broadcasted_iota(jnp.int32, (ny, nz), 1)
    row = lax.broadcasted_iota(jnp.int32, (ny, nz), 0)
    here = lax.rem(lax.div(lane, 2), nx)
    odd = lax.rem(lane, 2) == 1

    def clear(slot):
        got_g[slot] = jnp.zeros((4, ny, nz), F32)
        got_d[:, slot] = jnp.zeros((2, ny, nz), F32)
        got_q[slot] = jnp.zeros((ny, nz), F32)

    both(jnp.logical_not(not_top), lambda: clear(0))
    both(jnp.logical_not(not_last), lambda: clear(1))

    def pack(cells):
        packed = jnp.zeros((ny, nz), F32)
        for k, cell in enumerate(cells):
            packed = jnp.where(lax.div(lane, 2) == k, lane_roll(cell, 2 * k + 1), packed)
        return packed

    def sides(step, u):
        for c in range(nc):
            for x in range(nx):
                side_y[step, 0, c, x : x + 1] = u[c, x, ny - 1 : ny]
                side_y[step, 1, c, x : x + 1] = u[c, x, 0:1]

    def inner(u):
        none = jnp.zeros((nc, 1, ny, nz), F32)
        total = jnp.concatenate([u[:, 1:], none], axis=1) + jnp.concatenate([none, u[:, :-1]], axis=1)
        parts = []
        for c in range(nc):
            line = []
            for x in range(nx):
                cell = u[c, x]
                zs = jnp.where(lane == 0, 0.0, lane_roll(cell, 1)) + jnp.where(lane == nz - 1, 0.0, lane_roll(cell, -1))
                ys = jnp.where(row == 0, 0.0, row_roll(cell, 1)) + jnp.where(row == ny - 1, 0.0, row_roll(cell, -1))
                line.append(zs + ys)
            parts.append(jnp.stack(line))
        return total + jnp.stack(parts) - 6.0 * u

    def feeds(source):
        found = []
        for dx in (-1, 0, 1):
            for dy in (-1, 0, 1):
                if dx or dy:
                    found.append((dx, dy, source == ((here + dx) * ny + row + dy).astype(F32)))
        return found

    def fed_by(bottoms, masks):
        above = lane_roll(bottoms, 1)
        fed = above
        for dx, dy, mask in masks:
            moved = row_roll(above, -dy) if dy else above
            moved = lane_roll(moved, -2 * dx) if dx else moved
            fed = jnp.where(mask, moved, fed)
        return fed

    def ghost_tile(above, below, masks):
        return jnp.where(odd, fed_by(above, masks), lane_roll(below, -1))

    def ends(ghost, k, cell):
        moved = lane_roll(ghost, -(2 * k + 1))
        first = jnp.where(not_top, moved, cell)
        return jnp.where(lane == 0, first, jnp.where(lane == nz - 1, moved, 0.0))

    def rims(first, last):
        first = jnp.broadcast_to(first, (ny, nz))
        last = jnp.broadcast_to(last, (ny, nz))
        return jnp.where(row == 0, first, jnp.where(row == ny - 1, last, 0.0))

    def outer(step, u, ghost, before, after):
        parts = []
        for c in range(nc):
            line = []
            for x in range(nx):
                total = ends(ghost, c * nx + x, u[c, x])
                total = total + rims(got_y[step, 0, c, x : x + 1], got_y[step, 1, c, x : x + 1])
                if x == 0:
                    total = total + before[c]
                if x == nx - 1:
                    total = total + after[c]
                line.append(total)
            parts.append(jnp.stack(line))
        return jnp.stack(parts)

    loads[0].wait()
    u0 = u_v[:, 0]
    sides(0, u0)
    for e, x in ((0, 0), (1, nx - 1)):
        out_p[e, 0:nc] = u0[:, x]
        for c in range(nc):
            out_c[e, c : c + 1] = u0[c, x, ny - 1 : ny]
            out_c[e, nc + c : nc + c + 1] = u0[c, x, 0:1]
        out_c[e, 2 * nc :] = jnp.zeros((ny - 2 * nc, nz), F32)
    packed = pack([u0[c, x] for c in range(nc) for x in range(nx)])
    out_g[0] = packed
    for load in loads[1:5]:
        load.wait()
    mask = m_ref[0, 0, 0].astype(F32)
    stiff = k_v[0] * mask
    base = (2.0 * u0 - w_v[:, 0] + s_v[1, :, 0].astype(F32)) * mask + stiff[None] * inner(u0)
    own = i_v[0].astype(F32)
    spread = (lax.rem(lax.div(lax.broadcasted_iota(jnp.int32, (nz, nx), 0), 2), nx)
              == lax.broadcasted_iota(jnp.int32, (nz, nx), 1)).astype(F32)
    eye = (lax.broadcasted_iota(jnp.int32, (ny, ny), 0) == lax.broadcasted_iota(jnp.int32, (ny, ny), 1)).astype(F32)
    tall = jnp.dot(spread, own, preferred_element_type=F32)
    source = lax.dot_general(eye, tall, (((1,), (1,)), ((), ())), preferred_element_type=F32)
    for e, x in ((0, 0), (1, nx - 1)):
        out_p[e, nc : 2 * nc] = base[:, x]
        out_p[e, 2 * nc] = stiff[x]
        out_p[e, 2 * nc + 1] = source
    out_g[1] = pack([base[c, x] for c in range(nc) for x in range(nx)])
    out_g[2] = pack([stiff[x] for c in range(nc) for x in range(nx)])
    out_g[3] = source

    vertical_count = len(down)
    pl.semaphore_wait(barrier, 5 + vertical_count * (not_top.astype(jnp.int32) + not_last.astype(jnp.int32)))
    both(not_last, lambda: run(down, 6, "start"))
    both(not_top, lambda: run(up, 10, "start"))
    run(flat[:5], 0, "start")
    loads[5].wait()
    masks = feeds(source)
    run(flat[:5], 0, "wait_recv")
    both(not_top, lambda: run(down, 6, "wait_recv"))
    both(not_last, lambda: run(up, 10, "wait_recv"))

    ghost = ghost_tile(got_g[0, 0], got_g[1, 0], masks)
    u1 = base + stiff[None] * outer(0, u0, ghost, got_p[0, 0:nc], got_p[1, 0:nc])
    sides(1, u1)
    run(flat[5:], 5, "start")

    planes = []
    for e, x, beside in ((0, nx - 1, 0), (1, 0, nx - 1)):
        near = ghost_tile(got_d[e, 0], got_d[e, 1], feeds(got_p[e, 2 * nc + 1]))
        plane = []
        for c in range(nc):
            total = ends(near, c * nx + x, got_p[e, c]) + u0[c, beside]
            total = total + rims(got_c[e, c : c + 1], got_c[e, nc + c : nc + c + 1])
            plane.append(got_p[e, nc + c] + got_p[e, 2 * nc] * total)
        planes.append(plane)

    tiles = []
    for slot in range(2):
        if slot == 0:
            total = lane_roll(packed, -1)
        else:
            total = fed_by(packed, feeds(got_g[1, 3]))
        total = total + jnp.where(here == 0, lane_roll(got_d[0, slot], -2 * (nx - 1)), 0.0)
        total = total + jnp.where(here == nx - 1, lane_roll(got_d[1, slot], 2 * (nx - 1)), 0.0)
        total = total + jnp.where(row == 0, row_roll(got_q[slot], 1), 0.0)
        total = total + jnp.where(row == ny - 1, row_roll(got_q[slot], -1), 0.0)
        tiles.append(got_g[slot, 1] + got_g[slot, 2] * total)
    ghost = ghost_tile(tiles[0], tiles[1], masks)

    kern = jnp.sum(u1 * f_v[1, :, 0].astype(F32), axis=0)
    base = (2.0 * u1 - u0 + s_v[0, :, 0].astype(F32)) * mask + stiff[None] * inner(u1)
    run(flat[5:], 5, "wait_recv")
    u2 = base + stiff[None] * outer(1, u1, ghost, planes[0], planes[1])
    out_ref[:, 0] = u2
    kern_ref[0] = kern + jnp.sum(u2 * f_v[0, :, 0].astype(F32), axis=0)
    run(flat, 0, "wait_send")
    both(not_last, lambda: run(down, 6, "wait_send"))
    both(not_top, lambda: run(up, 10, "wait_send"))


def store(field_ref, kern_ref, field_out, kern_out, sem):
    first = pltpu.make_async_copy(field_ref, field_out, sem.at[0])
    second = pltpu.make_async_copy(kern_ref, kern_out, sem.at[1])
    first.start()
    second.start()
    first.wait()
    second.wait()


def solution(mesh):
    grids, patches = mesh.shape["grid"], mesh.shape["patch"]

    def local(now, prev, stiffness, source, forward, mask, feed):
        nc, _, nx, ny, nz = now.shape
        args = (now, prev, stiffness, source, forward, mask, feed)
        vmem = [pltpu.VMEM(a.shape, a.dtype) for a in args if a is not mask]
        tile = (ny, nz)
        return_shapes = (pltpu.VMEM(now.shape, F32), pltpu.VMEM(stiffness.shape, F32))
        done = pl.pallas_call(
            functools.partial(kernel, grids, patches),
            out_shape=return_shapes,
            in_specs=[pl.BlockSpec(memory_space=pltpu.HBM)] * 5
            + [pl.BlockSpec(memory_space=pltpu.SMEM), pl.BlockSpec(memory_space=pltpu.HBM)],
            out_specs=[pl.BlockSpec(memory_space=pltpu.VMEM)] * 2,
            scratch_shapes=vmem + [
                pltpu.VMEM((2, 2, nc, nx, nz), F32),
                pltpu.VMEM((2, 2 * nc + 2) + tile, F32),
                pltpu.VMEM((4,) + tile, F32),
                pltpu.VMEM((2,) + tile, F32),
                pltpu.VMEM((2, 2, nc, nx, nz), F32),
                pltpu.VMEM((2, 2 * nc + 2) + tile, F32),
                pltpu.VMEM((2, 4) + tile, F32),
                pltpu.VMEM((2, 2) + tile, F32),
                pltpu.VMEM((2,) + tile, F32),
                pltpu.VMEM((2,) + tile, F32),
                pltpu.SemaphoreType.DMA((6,)),
                pltpu.SemaphoreType.DMA((14,)),
                pltpu.SemaphoreType.DMA((14,)),
            ],
            compiler_params=pltpu.CompilerParams(collective_id=0, has_side_effects=True),
        )(*args)
        return pl.pallas_call(
            store,
            out_shape=(pltpu.HBM(now.shape, F32), pltpu.HBM(stiffness.shape, F32)),
            in_specs=[pl.BlockSpec(memory_space=pl.ANY)] * 2,
            out_specs=[pl.BlockSpec(memory_space=pltpu.HBM)] * 2,
            scratch_shapes=[pltpu.SemaphoreType.DMA((2,))],
        )(*[pltpu.with_memory_space_constraint(d, pltpu.VMEM) for d in done])

    in_specs = (
        P(None, "grid", "patch", "cross", None),
        P(None, "grid", "patch", "cross", None),
        P("grid", "patch", "cross", None),
        P(None, None, "grid", "patch", "cross", None),
        P(None, None, "grid", "patch", "cross", None),
        P("grid", "patch", "cross"),
        P("grid", "patch", "cross"),
    )
    out_specs = (P(None, "grid", "patch", "cross", None), P("grid", "patch", "cross", None))
    return jax.shard_map(local, mesh=mesh, in_specs=in_specs, out_specs=out_specs, check_vma=False)
```

```python
import functools

import jax
import jax.numpy as jnp
from jax import lax
from jax.experimental import pallas as pl
from jax.experimental.pallas import tpu as pltpu
from jax.sharding import PartitionSpec as P

MESH = pl.DeviceIdType.MESH
F32 = jnp.float32


def lane_roll(value, by):
    return pltpu.roll(value, by % value.shape[-1], value.ndim - 1)


def row_roll(value, by):
    return pltpu.roll(value, by % value.shape[-2], value.ndim - 2)


def kernel(
    grids, patches, u_hbm, w_hbm, k_hbm, s_hbm, f_hbm, m_ref, i_hbm, out_ref, kern_ref,
    u_v, i_v, k_v, w_v, s_v, f_v, side_y, out_p, out_g, out_c, got_y, got_p, got_g, got_d, got_q, got_c,
    load_sem, send_sem, recv_sem,
):
    g = lax.axis_index("grid")
    p = lax.axis_index("patch")
    q = lax.axis_index("cross")
    nxt = lax.rem(p + 1, patches)
    prv = lax.rem(p + patches - 1, patches)
    far = 1 - q
    not_top = g > 0
    not_last = g < grids - 1

    flat = (
        (out_p.at[1], got_p.at[0], (g, nxt, q)),
        (out_p.at[0], got_p.at[1], (g, prv, q)),
        (out_c.at[1], got_c.at[0], (g, nxt, far)),
        (out_c.at[0], got_c.at[1], (g, prv, far)),
        (side_y.at[0], got_y.at[0], (g, p, far)),
        (side_y.at[1], got_y.at[1], (g, p, far)),
    )

    def vertical(slot, other):
        return (
            (out_g, got_g.at[slot], (other, p, q)),
            (out_g.at[0], got_d.at[0, slot], (other, nxt, q)),
            (out_g.at[0], got_d.at[1, slot], (other, prv, q)),
            (out_g.at[0], got_q.at[slot], (other, p, far)),
        )

    down, up = vertical(0, g + 1), vertical(1, g - 1)

    def run(messages, first, what):
        for n, (src, dst, device) in enumerate(messages):
            copy = pltpu.make_async_remote_copy(
                src_ref=src, dst_ref=dst, send_sem=send_sem.at[first + n], recv_sem=recv_sem.at[first + n],
                device_id=device, device_id_type=MESH,
            )
            getattr(copy, what)()

    barrier = pltpu.get_barrier_semaphore()

    def greet(messages):
        for _, _, device in messages:
            pl.semaphore_signal(barrier, inc=1, device_id=device, device_id_type=MESH)

    def both(condition, body):
        @pl.when(condition)
        def _():
            body()

    pairs = ((u_hbm, u_v), (i_hbm, i_v), (k_hbm, k_v), (w_hbm, w_v), (s_hbm, s_v), (f_hbm, f_v))
    loads = [pltpu.make_async_copy(a, b, load_sem.at[n]) for n, (a, b) in enumerate(pairs)]
    for load in loads:
        load.start()

    greet(flat[:5])
    both(not_last, lambda: greet(down))
    both(not_top, lambda: greet(up))

    nc, nx, ny, nz = u_v.shape[0], u_v.shape[2], u_v.shape[3], u_v.shape[4]
    lane = lax.broadcasted_iota(jnp.int32, (ny, nz), 1)
    row = lax.broadcasted_iota(jnp.int32, (ny, nz), 0)
    here = lax.rem(lax.div(lane, 2), nx)
    odd = lax.rem(lane, 2) == 1

    def clear(slot):
        got_g[slot] = jnp.zeros((4, ny, nz), F32)
        got_d[:, slot] = jnp.zeros((2, ny, nz), F32)
        got_q[slot] = jnp.zeros((ny, nz), F32)

    both(jnp.logical_not(not_top), lambda: clear(0))
    both(jnp.logical_not(not_last), lambda: clear(1))

    def pack(cells):
        packed = jnp.zeros((ny, nz), F32)
        for k, cell in enumerate(cells):
            packed = jnp.where(lax.div(lane, 2) == k, lane_roll(cell, 2 * k + 1), packed)
        return packed

    def sides(step, u):
        for c in range(nc):
            for x in range(nx):
                side_y[step, 0, c, x : x + 1] = u[c, x, ny - 1 : ny]
                side_y[step, 1, c, x : x + 1] = u[c, x, 0:1]

    def inner(u):
        none = jnp.zeros((nc, 1, ny, nz), F32)
        total = jnp.concatenate([u[:, 1:], none], axis=1) + jnp.concatenate([none, u[:, :-1]], axis=1)
        parts = []
        for c in range(nc):
            line = []
            for x in range(nx):
                cell = u[c, x]
                zs = jnp.where(lane == 0, 0.0, lane_roll(cell, 1)) + jnp.where(lane == nz - 1, 0.0, lane_roll(cell, -1))
                ys = jnp.where(row == 0, 0.0, row_roll(cell, 1)) + jnp.where(row == ny - 1, 0.0, row_roll(cell, -1))
                line.append(zs + ys)
            parts.append(jnp.stack(line))
        return total + jnp.stack(parts) - 6.0 * u

    def feeds(source):
        found = []
        for dx in (-1, 0, 1):
            for dy in (-1, 0, 1):
                if dx or dy:
                    found.append((dx, dy, source == ((here + dx) * ny + row + dy).astype(F32)))
        return found

    def fed_by(bottoms, masks):
        above = lane_roll(bottoms, 1)
        fed = above
        for dx, dy, mask in masks:
            moved = row_roll(above, -dy) if dy else above
            moved = lane_roll(moved, -2 * dx) if dx else moved
            fed = jnp.where(mask, moved, fed)
        return fed

    def ghost_tile(above, below, masks):
        return jnp.where(odd, fed_by(above, masks), lane_roll(below, -1))

    def ends(ghost, k, cell):
        moved = lane_roll(ghost, -(2 * k + 1))
        first = jnp.where(not_top, moved, cell)
        return jnp.where(lane == 0, first, jnp.where(lane == nz - 1, moved, 0.0))

    def rims(first, last):
        first = jnp.broadcast_to(first, (ny, nz))
        last = jnp.broadcast_to(last, (ny, nz))
        return jnp.where(row == 0, first, jnp.where(row == ny - 1, last, 0.0))

    def outer(step, u, ghost, before, after):
        parts = []
        for c in range(nc):
            line = []
            for x in range(nx):
                total = ends(ghost, c * nx + x, u[c, x])
                total = total + rims(got_y[step, 0, c, x : x + 1], got_y[step, 1, c, x : x + 1])
                if x == 0:
                    total = total + before[c]
                if x == nx - 1:
                    total = total + after[c]
                line.append(total)
            parts.append(jnp.stack(line))
        return jnp.stack(parts)

    loads[0].wait()
    u0 = u_v[:, 0]
    sides(0, u0)
    for e, x in ((0, 0), (1, nx - 1)):
        out_p[e, 0:nc] = u0[:, x]
        for c in range(nc):
            out_c[e, c : c + 1] = u0[c, x, ny - 1 : ny]
            out_c[e, nc + c : nc + c + 1] = u0[c, x, 0:1]
        out_c[e, 2 * nc :] = jnp.zeros((ny - 2 * nc, nz), F32)
    packed = pack([u0[c, x] for c in range(nc) for x in range(nx)])
    out_g[0] = packed
    loads[1].wait()
    own = i_v[0].astype(F32)
    spread = (lax.rem(lax.div(lax.broadcasted_iota(jnp.int32, (nz, nx), 0), 2), nx)
              == lax.broadcasted_iota(jnp.int32, (nz, nx), 1)).astype(F32)
    eye = (lax.broadcasted_iota(jnp.int32, (ny, ny), 0) == lax.broadcasted_iota(jnp.int32, (ny, ny), 1)).astype(F32)
    tall = jnp.dot(spread, own, preferred_element_type=F32)
    source = lax.dot_general(eye, tall, (((1,), (1,)), ((), ())), preferred_element_type=F32)
    out_g[3] = source
    loads[2].wait()
    mask = m_ref[0, 0, 0].astype(F32)
    stiff = k_v[0] * mask
    third = pack([stiff[x] for x in range(nx)])
    out_g[2] = third + lane_roll(third, 2 * nx) + lane_roll(third, 4 * nx)
    rest = stiff[None] * inner(u0)
    loads[3].wait()
    loads[4].wait()
    base = (2.0 * u0 - w_v[:, 0] + s_v[1, :, 0].astype(F32)) * mask + rest
    for e, x in ((0, 0), (1, nx - 1)):
        out_p[e, nc : 2 * nc] = base[:, x]
        out_p[e, 2 * nc] = stiff[x]
        out_p[e, 2 * nc + 1] = source
    out_g[1] = pack([base[c, x] for c in range(nc) for x in range(nx)])

    vertical_count = len(down)
    pl.semaphore_wait(barrier, 5 + vertical_count * (not_top.astype(jnp.int32) + not_last.astype(jnp.int32)))
    both(not_last, lambda: run(down, 6, "start"))
    both(not_top, lambda: run(up, 10, "start"))
    run(flat[:5], 0, "start")
    loads[5].wait()
    masks = feeds(source)
    run(flat[:5], 0, "wait_recv")
    both(not_top, lambda: run(down, 6, "wait_recv"))
    both(not_last, lambda: run(up, 10, "wait_recv"))

    ghost = ghost_tile(got_g[0, 0], got_g[1, 0], masks)
    u1 = base + stiff[None] * outer(0, u0, ghost, got_p[0, 0:nc], got_p[1, 0:nc])
    sides(1, u1)
    run(flat[5:], 5, "start")

    planes = []
    for e, x, beside in ((0, nx - 1, 0), (1, 0, nx - 1)):
        near = ghost_tile(got_d[e, 0], got_d[e, 1], feeds(got_p[e, 2 * nc + 1]))
        plane = []
        for c in range(nc):
            total = ends(near, c * nx + x, got_p[e, c]) + u0[c, beside]
            total = total + rims(got_c[e, c : c + 1], got_c[e, nc + c : nc + c + 1])
            plane.append(got_p[e, nc + c] + got_p[e, 2 * nc] * total)
        planes.append(plane)

    tiles = []
    for slot in range(2):
        if slot == 0:
            total = lane_roll(packed, -1)
        else:
            total = fed_by(packed, feeds(got_g[1, 3]))
        total = total + jnp.where(here == 0, lane_roll(got_d[0, slot], -2 * (nx - 1)), 0.0)
        total = total + jnp.where(here == nx - 1, lane_roll(got_d[1, slot], 2 * (nx - 1)), 0.0)
        total = total + jnp.where(row == 0, row_roll(got_q[slot], 1), 0.0)
        total = total + jnp.where(row == ny - 1, row_roll(got_q[slot], -1), 0.0)
        tiles.append(got_g[slot, 1] + got_g[slot, 2] * total)
    ghost = ghost_tile(tiles[0], tiles[1], masks)

    kern = jnp.sum(u1 * f_v[1, :, 0].astype(F32), axis=0)
    base = (2.0 * u1 - u0 + s_v[0, :, 0].astype(F32)) * mask + stiff[None] * inner(u1)
    run(flat[5:], 5, "wait_recv")
    u2 = base + stiff[None] * outer(1, u1, ghost, planes[0], planes[1])
    out_ref[:, 0] = u2
    kern_ref[0] = kern + jnp.sum(u2 * f_v[0, :, 0].astype(F32), axis=0)
    run(flat, 0, "wait_send")
    both(not_last, lambda: run(down, 6, "wait_send"))
    both(not_top, lambda: run(up, 10, "wait_send"))


def store(field_ref, kern_ref, field_out, kern_out, sem):
    first = pltpu.make_async_copy(field_ref, field_out, sem.at[0])
    second = pltpu.make_async_copy(kern_ref, kern_out, sem.at[1])
    first.start()
    second.start()
    first.wait()
    second.wait()


def solution(mesh):
    grids, patches = mesh.shape["grid"], mesh.shape["patch"]

    def local(now, prev, stiffness, source, forward, mask, feed):
        nc, _, nx, ny, nz = now.shape
        args = (now, prev, stiffness, source, forward, mask, feed)
        vmem = [pltpu.VMEM(a.shape, a.dtype) for a in args if a is not mask]
        vmem = [vmem[n] for n in (0, 5, 2, 1, 3, 4)]
        tile = (ny, nz)
        return_shapes = (pltpu.VMEM(now.shape, F32), pltpu.VMEM(stiffness.shape, F32))
        done = pl.pallas_call(
            functools.partial(kernel, grids, patches),
            out_shape=return_shapes,
            in_specs=[pl.BlockSpec(memory_space=pltpu.HBM)] * 5
            + [pl.BlockSpec(memory_space=pltpu.SMEM), pl.BlockSpec(memory_space=pltpu.HBM)],
            out_specs=[pl.BlockSpec(memory_space=pltpu.VMEM)] * 2,
            scratch_shapes=vmem + [
                pltpu.VMEM((2, 2, nc, nx, nz), F32),
                pltpu.VMEM((2, 2 * nc + 2) + tile, F32),
                pltpu.VMEM((4,) + tile, F32),
                pltpu.VMEM((2,) + tile, F32),
                pltpu.VMEM((2, 2, nc, nx, nz), F32),
                pltpu.VMEM((2, 2 * nc + 2) + tile, F32),
                pltpu.VMEM((2, 4) + tile, F32),
                pltpu.VMEM((2, 2) + tile, F32),
                pltpu.VMEM((2,) + tile, F32),
                pltpu.VMEM((2,) + tile, F32),
                pltpu.SemaphoreType.DMA((6,)),
                pltpu.SemaphoreType.DMA((14,)),
                pltpu.SemaphoreType.DMA((14,)),
            ],
            compiler_params=pltpu.CompilerParams(collective_id=0, has_side_effects=True),
        )(*args)
        return pl.pallas_call(
            store,
            out_shape=(pltpu.HBM(now.shape, F32), pltpu.HBM(stiffness.shape, F32)),
            in_specs=[pl.BlockSpec(memory_space=pl.ANY)] * 2,
            out_specs=[pl.BlockSpec(memory_space=pltpu.HBM)] * 2,
            scratch_shapes=[pltpu.SemaphoreType.DMA((2,))],
        )(*[pltpu.with_memory_space_constraint(d, pltpu.VMEM) for d in done])

    in_specs = (
        P(None, "grid", "patch", "cross", None),
        P(None, "grid", "patch", "cross", None),
        P("grid", "patch", "cross", None),
        P(None, None, "grid", "patch", "cross", None),
        P(None, None, "grid", "patch", "cross", None),
        P("grid", "patch", "cross"),
        P("grid", "patch", "cross"),
    )
    out_specs = (P(None, "grid", "patch", "cross", None), P("grid", "patch", "cross", None))
    return jax.shard_map(local, mesh=mesh, in_specs=in_specs, out_specs=out_specs, check_vma=False)
```
